32 devices in a mesh: dom: 16 (over z, y, core), sub: 2 (over x).
Axes of the slice: x: 2, y: 2, z: 4, core: 2. Of those that a mesh axis runs over, the one named last changes fastest.
Arguments:
- dof_state: float32 [56, 9, 4096], P(None, None, ('dom', 'sub')), may hold values from -6 to 6
- stiffness: float32 [3, 56, 56], replicated, may hold values from -0.75 to 0.75
- face_proj: float32 [4, 21, 56], replicated, may hold values from -0.75 to 0.75
- face_lift: float32 [4, 56, 21], replicated, may hold values from -1 to 1
- face_rotate: float32 [3, 21, 21], replicated, may hold values from -1.25 to 1.25
- jacobians: float32 [16, 3, 9, 9], replicated, may hold values from -2 to 2
- material: int32 [4096], P(('dom', 'sub')), may hold values from 0 to 15
- inv_jacobian: float32 [3, 3, 4096], P(None, None, ('dom', 'sub')), may hold values from -2.5 to 2.5
- flux_own: float32 [4, 9, 9, 4096], P(None, None, None, ('dom', 'sub')), may hold values from -1.5 to 1.5
- flux_across: float32 [4, 9, 9, 4096], P(None, None, None, ('dom', 'sub')), may hold values from -1.5 to 1.5
- cluster: int32 [4096], P(('dom', 'sub')), may hold values from 0 to 1, as said below
- neighbour: int32 [4, 4096], P(None, ('dom', 'sub')), may hold values from 0 to 176, as said below
- across_face: int32 [4, 4096], P(None, ('dom', 'sub')), may hold values from 0 to 3
- rotation: int32 [4, 4096], P(None, ('dom', 'sub')), may hold values from 0 to 2
- send_list: int32 [1536], P(('dom', 'sub')), may hold values from 0 to 127
Outputs:
- dof_out: float32 [56, 9, 4096], P(None, None, ('dom', 'sub'))
The draws below stay inside these ranges and needn't reach their ends.
Inputs may be any that keep to these rules, and one draw needn't show every extreme that they name: `cluster`: each partition of 128 elements has at most 64 fine elements, and some partition has exactly 64. `neighbour`: values below 128 are the partition's own elements, never the element itself; 128 + g is received slot g; 176 is an outflow face. Every received slot whose source partition exists is named by exactly one face of the partition.
All inputs are finite; a program needn't handle non-finite values.
Results may differ from the reference program's by a relative error of at most 0.0003.
Values sent between devices are 32-bit elements; how exact they have to be, the bound alone decides.
A program may use at most 64 MiB of HBM per device.

```python
import math
import jax
import jax.numpy as jnp
from jax import lax

NB = 56
NF = 9
FB = 21
ORDER = 6
NMAT = 16
EL = 128
BLK = 8
FINE_MAX = 64
SUBS = 2
SLABS = 16
PARTS_SIZE = 32
GHOSTS = 48
ELEMENTS = 4096


def cluster_ids(key):
    base_key = jax.random.fold_in(key, 101)
    count_key, busy_key, order_key = jax.random.split(base_key, 3)
    raw_counts = jax.random.randint(count_key, (PARTS_SIZE,), 0, FINE_MAX + 1)
    counts = raw_counts * raw_counts // FINE_MAX
    busiest = jax.random.randint(busy_key, (), 0, PARTS_SIZE)
    counts = jnp.where(jnp.arange(PARTS_SIZE) == busiest, FINE_MAX, counts)
    rank_table = jax.vmap(lambda one_key: jax.random.permutation(one_key, EL))(jax.random.split(order_key, PARTS_SIZE))
    labels = jnp.where(rank_table < counts[:, None], 0, 1).astype(jnp.int32)
    return labels.reshape(PARTS_SIZE * EL)


def draw_cluster(key, part):
    return cluster_ids(key)


def draw_inv_jacobian(key, part):
    labels = cluster_ids(key)
    step_scale = jnp.where(labels == 0, 1.0, 0.5).astype(jnp.float32)
    noise_key, factor_key = jax.random.split(jax.random.fold_in(key, 202))
    identity = jnp.eye(3, dtype=jnp.float32)[:, :, None]
    noise = jax.random.truncated_normal(noise_key, -3.0, 3.0, (3, 3, ELEMENTS), jnp.float32)
    factor = jnp.exp(jax.random.uniform(factor_key, (ELEMENTS,), jnp.float32, math.log(0.7), math.log(1.4)))
    return (step_scale * factor)[None, None, :] * (0.5 * identity + 0.35 * noise)


def draw_neighbour(key, part):

    def one_part(part_key, partition):
        local_key, place_key = jax.random.split(part_key)
        slab = partition // SUBS
        sub_pos = partition % SUBS
        slots = jnp.arange(GHOSTS, dtype=jnp.int32)
        peer_slot = slots // BLK
        slab_step = peer_slot // SUBS - 1
        peer_sub = peer_slot % SUBS
        exists = (slab + slab_step >= 0) & (slab + slab_step < SLABS) & jnp.logical_not((slab_step == 0) & (peer_sub == sub_pos))
        outflow = EL + GHOSTS
        ghost_values = jnp.where(exists, EL + slots, outflow)
        face_count = 4 * EL
        positions = jnp.arange(face_count, dtype=jnp.int32)
        owners = positions % EL
        inside = (owners + 1 + jax.random.randint(local_key, (face_count,), 0, EL - 1)) % EL
        placement = jax.random.permutation(place_key, face_count)
        values = jnp.where(placement < GHOSTS, ghost_values[jnp.minimum(placement, GHOSTS - 1)], jnp.where(placement < GHOSTS + EL // 8, outflow, inside))
        return values.reshape(4, EL).astype(jnp.int32)
    part_keys = jax.random.split(jax.random.fold_in(key, 303), PARTS_SIZE)
    every_part = jax.vmap(one_part)(part_keys, jnp.arange(PARTS_SIZE, dtype=jnp.int32))
    return jnp.transpose(every_part, (1, 0, 2)).reshape(4, ELEMENTS)


def place_ends(values, rng, low, largest):
    place = [jax.random.randint(jax.random.fold_in(rng, axis), (), 0, length) for axis, length in enumerate(values.shape)]
    main_axis = values.shape.index(max(values.shape))
    beside = place[:main_axis] + [(place[main_axis] + 1) % values.shape[main_axis]] + place[main_axis + 1:]
    return values.at[tuple(place)].set(low).at[tuple(beside)].set(largest)


def block_scale(rng, dims, cuts, smallest, largest):
    level, own = 1.0, jax.random.fold_in(rng, 6)
    for position, blocks in cuts:
        draws = jnp.exp(jax.random.uniform(jax.random.fold_in(own, position), (blocks,), jnp.float32, smallest / len(cuts), largest / len(cuts)))
        level = level * jnp.repeat(draws, dims[position] // blocks).reshape([-1 if axis == position else 1 for axis in range(len(dims))])
    return level


def normal_values(key, shape, spread, most, cuts=(), held_as=jnp.bfloat16):
    drawn = jax.random.normal(key, shape, jnp.float32) * spread
    if len(cuts) > 0:
        drawn = block_scale(key, shape, cuts, -0.22, 0.18) * drawn
    return jnp.clip(drawn, min=-most, max=most).astype(held_as)


def setup_inputs(seed: int = 0) -> dict:
    key_list = jax.random.split(jax.random.key(seed), 16)
    dof_state = normal_values(key_list[0], (NB, NF, ELEMENTS), 1.0, 6.0, ((2, 32),), jnp.float32)
    stiffness = normal_values(key_list[1], (3, NB, NB), NB ** -0.5, 0.75, (), jnp.float32)
    face_proj = normal_values(key_list[2], (4, FB, NB), NB ** -0.5, 0.75, (), jnp.float32)
    face_lift = normal_values(key_list[3], (4, NB, FB), (2 * FB) ** -0.5, 1.0, (), jnp.float32)
    face_rotate = normal_values(key_list[4], (3, FB, FB), FB ** -0.5, 1.25, (), jnp.float32)
    jacobians = normal_values(key_list[5], (NMAT, 3, NF, NF), NF ** -0.5, 2.0, (), jnp.float32)
    material = place_ends(jax.random.randint(key_list[6], (ELEMENTS,), 0, NMAT), jax.random.fold_in(key_list[6], 1), 0, NMAT - 1).astype(jnp.int32)
    inv_jacobian = draw_inv_jacobian(jax.random.fold_in(key_list[15], 71), 0)
    flux_own = normal_values(key_list[8], (4, NF, NF, ELEMENTS), (2 * NF) ** -0.5, 1.5, ((3, 32),), jnp.float32)
    flux_across = normal_values(key_list[9], (4, NF, NF, ELEMENTS), (2 * NF) ** -0.5, 1.5, ((3, 32),), jnp.float32)
    cluster = draw_cluster(jax.random.fold_in(key_list[15], 71), 0)
    neighbour = draw_neighbour(jax.random.fold_in(key_list[15], 71), 0)
    across_face = place_ends(jax.random.randint(key_list[12], (4, ELEMENTS), 0, 4), jax.random.fold_in(key_list[12], 1), 0, 3).astype(jnp.int32)
    rotation = place_ends(jax.random.randint(key_list[13], (4, ELEMENTS), 0, 3), jax.random.fold_in(key_list[13], 1), 0, 2).astype(jnp.int32)
    send_list = place_ends(jax.random.randint(key_list[14], (PARTS_SIZE * GHOSTS,), 0, EL), jax.random.fold_in(key_list[14], 1), 0, EL - 1).astype(jnp.int32)
    return dict(dof_state=dof_state, stiffness=stiffness, face_proj=face_proj, face_lift=face_lift, face_rotate=face_rotate, jacobians=jacobians, material=material, inv_jacobian=inv_jacobian, flux_own=flux_own, flux_across=flux_across, cluster=cluster, neighbour=neighbour, across_face=across_face, rotation=rotation, send_list=send_list)


HIGH = lax.Precision.HIGHEST


def mix_fields(data, mats):
    return jnp.sum(data[:, :, None, :] * mats[None], axis=1)


def star_of(inv_jacobian, jacobians, material):
    nmat = jacobians.shape[0]
    fields = jacobians.shape[2]
    picked = (material[None, :] == jnp.arange(nmat, dtype=jnp.int32)[:, None]).astype(jnp.float32)
    table = jnp.transpose(jacobians.reshape(nmat, 3 * fields * fields))
    per_elem = jnp.dot(table, picked, precision=HIGH).reshape(3, fields, fields, material.shape[0])
    stacked = []
    for dim_d in range(3):
        summed = inv_jacobian[0, dim_d][None, None, :] * per_elem[0]
        for dim_c in range(1, 3):
            summed = summed + inv_jacobian[dim_c, dim_d][None, None, :] * per_elem[dim_c]
        stacked.append(summed)
    return jnp.stack(stacked)


def derivative(state, stiffness, star_mats):
    total = None
    for dim_d in range(3):
        moved = jnp.einsum('xb,xqe->bqe', stiffness[dim_d], state, precision=HIGH)
        term = mix_fields(moved, star_mats[dim_d])
        total = term if total is None else total + term
    return -total


def taylor(state, stiffness, star_mats):
    series = [state]
    for order in range(ORDER - 1):
        series.append(derivative(series[-1], stiffness, star_mats))
    return series


def integral(series, start_time, end_time):
    summed = jnp.zeros_like(series[0])
    for order in range(len(series)):
        factor = (end_time ** (order + 1) - start_time ** (order + 1)) / math.factorial(order + 1)
        summed = summed + factor * series[order]
    return summed


def volume(own_integral, stiffness, star_mats):
    total = None
    for dim_d in range(3):
        weighted = mix_fields(own_integral, star_mats[dim_d])
        term = jnp.einsum('bx,xpe->bpe', stiffness[dim_d], weighted, precision=HIGH)
        total = term if total is None else total + term
    return total


def lift_faces(solved_list, face_lift):
    faces, basis, face_basis = face_lift.shape
    lifter = jnp.transpose(face_lift, (1, 0, 2)).reshape(basis, faces * face_basis)
    return jnp.einsum('bg,gpe->bpe', lifter, jnp.concatenate(solved_list, axis=0), precision=HIGH)


def local_faces(own_integral, face_proj, face_lift, flux_own):
    faces, face_basis, basis = face_proj.shape
    projected = jnp.einsum('gx,xqe->gqe', face_proj.reshape(faces * face_basis, basis), own_integral, precision=HIGH)
    solved_list = [mix_fields(projected[i * face_basis:(i + 1) * face_basis], flux_own[i]) for i in range(faces)]
    return lift_faces(solved_list, face_lift)


def neighbour_faces(near_list, across_face, rotation, face_proj, face_lift, face_rotate, flux_across):
    faces, face_basis, basis = face_proj.shape
    combos = jnp.einsum('hfg,jgx->hjfx', face_rotate, face_proj, precision=HIGH).reshape(12 * face_basis, basis)
    solved_list = []
    for i in range(faces):
        near = near_list[i]
        projected = jnp.einsum('gx,xqe->gqe', combos, near, precision=HIGH)
        projected = projected.reshape(12, face_basis, near.shape[1], near.shape[2])
        choice_key = rotation[i] * 4 + across_face[i]
        pick = (choice_key[None, :] == jnp.arange(12, dtype=jnp.int32)[:, None]).astype(jnp.float32)
        chosen = jnp.sum(projected * pick[:, None, None, :], axis=0)
        solved_list.append(mix_fields(chosen, flux_across[i]))
    return lift_faces(solved_list, face_lift)


def update(base_state, own_integral, near_list, stiffness, star_mats, face_proj, face_lift, face_rotate,
           flux_own, flux_across, across_face, rotation):
    result = base_state + volume(own_integral, stiffness, star_mats)
    result = result - local_faces(own_integral, face_proj, face_lift, flux_own)
    return result - neighbour_faces(near_list, across_face, rotation, face_proj, face_lift, face_rotate, flux_across)


def neighbour_sources(neighbour, send_list):
    partition = jnp.arange(PARTS_SIZE, dtype=jnp.int32)[:, None]
    slots = jnp.arange(GHOSTS, dtype=jnp.int32)[None, :]
    peer_slot = slots // BLK
    member = slots % BLK
    slab_step = peer_slot // SUBS - 1
    peer_sub = peer_slot % SUBS
    slab = partition // SUBS
    sub_pos = partition % SUBS
    exists = (slab + slab_step >= 0) & (slab + slab_step < SLABS) & jnp.logical_not((slab_step == 0) & (peer_sub == sub_pos))
    peer = jnp.clip((slab + slab_step) * SUBS + peer_sub, 0, PARTS_SIZE - 1)
    back_block = (1 - slab_step) * SUBS + sub_pos
    listed = send_list[peer * GHOSTS + back_block * BLK + member]
    ghost_src = jnp.where(exists, peer * EL + listed, ELEMENTS).astype(jnp.int32)
    owners = jnp.broadcast_to((jnp.arange(ELEMENTS, dtype=jnp.int32) // EL)[None, :], neighbour.shape)
    ghost_pick = ghost_src[owners, jnp.clip(neighbour - EL, 0, GHOSTS - 1)]
    inside = neighbour < EL
    received = (neighbour >= EL) & (neighbour < EL + GHOSTS)
    return jnp.where(inside, owners * EL + neighbour, jnp.where(received, ghost_pick, ELEMENTS)).astype(jnp.int32)


def to_blocks(array):
    lead = array.shape[:-1]
    return jnp.moveaxis(array.reshape(lead + (SLABS, SUBS * EL)), -2, 0)


def from_blocks(array):
    moved_back = jnp.moveaxis(array, 0, -2)
    return moved_back.reshape(moved_back.shape[:-2] + (ELEMENTS,))


def reference(dof_state, stiffness, face_proj, face_lift, face_rotate, jacobians, material, inv_jacobian,
              flux_own, flux_across, cluster, neighbour, across_face, rotation, send_list):
    sources = neighbour_sources(neighbour, send_list)
    state_blocks = to_blocks(dof_state)
    inv_blocks = to_blocks(inv_jacobian)
    mat_blocks = to_blocks(material)
    own_blocks = to_blocks(flux_own)
    across_blocks = to_blocks(flux_across)
    source_blocks = to_blocks(sources)
    face_blocks = to_blocks(across_face)
    turn_blocks = to_blocks(rotation)
    cluster_blocks = to_blocks(cluster)
    zero_column = jnp.zeros((NB, NF, 1), dof_state.dtype)

    def predict_block(pieces):
        state_block, inv_block, mat_block = pieces
        star_mats = star_of(inv_block, jacobians, mat_block)
        series = taylor(state_block, stiffness, star_mats)
        return integral(series, 0.0, 1.0), integral(series, 1.0, 2.0)

    first_blocks, second_blocks = lax.map(predict_block, (state_blocks, inv_blocks, mat_blocks))
    padded_first = jnp.concatenate([from_blocks(first_blocks), zero_column], axis=2)

    def fine_block(pieces):
        (state_block, first_block, second_block, inv_block, mat_block, own_block, across_block,
         source_block, face_block, turn_block, cluster_block) = pieces
        star_mats = star_of(inv_block, jacobians, mat_block)
        near_list = [jnp.take(padded_first, source_block[i], axis=2) for i in range(4)]
        stepped = update(state_block, first_block, near_list, stiffness, star_mats, face_proj, face_lift,
                         face_rotate, own_block, across_block, face_block, turn_block)
        second_step = integral(taylor(stepped, stiffness, star_mats), 0.0, 1.0)
        is_fine = cluster_block == 0
        later_half = jnp.where(is_fine, second_step, second_block)
        base_state = jnp.where(is_fine, stepped, state_block)
        own_integral = jnp.where(is_fine, second_step, first_block + second_block)
        return later_half, base_state, own_integral

    later_blocks, base_blocks, integral_blocks = lax.map(
        fine_block, (state_blocks, first_blocks, second_blocks, inv_blocks, mat_blocks, own_blocks,
                     across_blocks, source_blocks, face_blocks, turn_blocks, cluster_blocks))
    padded_later = jnp.concatenate([from_blocks(later_blocks), zero_column], axis=2)

    def final_block(pieces):
        (base_block, integral_block, inv_block, mat_block, own_block, across_block, source_block,
         face_block, turn_block, cluster_block) = pieces
        star_mats = star_of(inv_block, jacobians, mat_block)
        is_fine = (cluster_block == 0)[None, None, :]
        near_list = []
        for i in range(4):
            near_first = jnp.take(padded_first, source_block[i], axis=2)
            near_later = jnp.take(padded_later, source_block[i], axis=2)
            near_list.append(jnp.where(is_fine, near_later, near_first + near_later))
        return update(base_block, integral_block, near_list, stiffness, star_mats, face_proj, face_lift,
                      face_rotate, own_block, across_block, face_block, turn_block)

    out_blocks = lax.map(final_block, (base_blocks, integral_blocks, inv_blocks, mat_blocks, own_blocks,
                                       across_blocks, source_blocks, face_blocks, turn_blocks, cluster_blocks))
    return from_blocks(out_blocks)
```

```python
import functools
import math

import jax
import jax.numpy as jnp
from jax import lax
from jax.experimental import pallas as pl
from jax.experimental.pallas import tpu as pltpu
from jax.sharding import PartitionSpec as P

ORDER = 6
MESH = pl.DeviceIdType.MESH
F32 = jnp.float32
BF16 = jnp.bfloat16


def split(x):
    hi = x.astype(BF16)
    return hi, (x - hi.astype(F32)).astype(BF16)


def tripled(x):
    hi, lo = split(x)
    return jnp.concatenate([hi, lo, hi], axis=0)


def grown(x, rows):
    if x.shape[0] == rows:
        return x
    return jnp.concatenate([x, jnp.zeros((rows - x.shape[0], x.shape[1]), x.dtype)], axis=0)


def weights(x, depth):
    x = grown(x, depth)
    w = jnp.transpose(jnp.concatenate([x, x, x], axis=0))
    hi, lo = split(w)
    lane = lax.broadcasted_iota(jnp.int32, w.shape, 1)
    return jnp.where(lane < 2 * depth, hi.astype(F32), lo.astype(F32)).astype(BF16)


def dot(a, b):
    return jnp.dot(a, b, preferred_element_type=F32)


def kernel(dims, *refs):
    hbm, refs = refs[:15], refs[15:]
    out_ref, held, refs = refs[0], refs[1:16], refs[16:]
    (
        dof_ref,
        stiff_ref,
        proj_ref,
        lift_ref,
        rot_ref,
        table_ref,
        inv_ref,
        own_ref,
        across_ref,
        material_ref,
        cluster_ref,
        neighbour_ref,
        face_ref,
        turn_ref,
        send_ref,
    ) = held
    (
        sendbuf,
        ghost,
        star,
        state,
        moved,
        proj,
        first,
        second,
        stepped,
        chosen,
        chosen_first,
        solved,
        onehot,
        send_sem,
        recv_sem,
        load_sem,
    ) = refs
    loads = [
        pltpu.make_async_copy(hbm[k], held[k], load_sem.at[k]) for k in range(15)
    ]
    for k in (5, 9, 6, 1, 0, 14, 10, 2, 11, 12, 13, 7, 3, 4, 8):
        loads[k].start()

    def ready(*which):
        for k in which:
            loads[k].wait()

    nb, nf, el, fp, nfaces, slabs, subs, blk = dims
    kb = state.shape[1]
    peers = 3 * subs
    slots = peers * blk
    slab = lax.axis_index("dom")
    sub = lax.axis_index("sub")
    barrier = pltpu.get_barrier_semaphore()

    def each_peer(act):
        for t in (-1, 0, 1):
            for r in range(subs):
                there = slab + t
                valid = (there >= 0) & (there < slabs)
                if t == 0:
                    valid = valid & (sub != r)

                @pl.when(valid)
                def _(t=t, r=r, there=there):
                    act(t, r, there)

    ghost[...] = jnp.zeros(ghost.shape, F32)
    each_peer(
        lambda t, r, there: pl.semaphore_signal(
            barrier, inc=1, device_id=(there, r), device_id_type=MESH
        )
    )

    def copy_to(x, t, r, there):
        slot = (1 - t) * subs + sub
        return pltpu.make_async_remote_copy(
            src_ref=sendbuf.at[x, (t + 1) * subs + r],
            dst_ref=ghost.at[x, slot],
            send_sem=send_sem.at[x, (t + 1) * subs + r],
            recv_sem=recv_sem.at[x, slot],
            device_id=(there, r),
            device_id_type=MESH,
        )

    def arrival(x, t, r, there):
        j = (t + 1) * subs + r
        return pltpu.make_async_remote_copy(
            src_ref=sendbuf.at[x, j],
            dst_ref=ghost.at[x, j],
            send_sem=send_sem.at[x, j],
            recv_sem=recv_sem.at[x, j],
            device_id=(there, r),
            device_id_type=MESH,
        )

    ready(5, 9, 6)
    nmat = table_ref.shape[3]
    rows = lax.broadcasted_iota(jnp.int32, (nmat, el), 0)
    picked = (rows == material_ref[...]).astype(F32).astype(BF16)
    per_elem = []
    for c in range(3):
        hi, lo = split(table_ref[:, :, c, :].reshape(nf * nf, nmat))
        per_elem.append(dot(hi, picked) + dot(lo, picked))
    for d in range(3):
        total = inv_ref[0, d : d + 1, :] * per_elem[0]
        for c in range(1, 3):
            total = total + inv_ref[c, d : d + 1, :] * per_elem[c]
        star[d] = jnp.broadcast_to(total[:, None, :], (nf * nf, 8, el))

    ready(1, 0, 14, 10, 2, 11, 12, 13, 7, 3, 4, 8)
    onerow = lax.broadcasted_iota(jnp.int32, (4 * el, el), 0)
    for i in range(nfaces):
        n = neighbour_ref[i : i + 1, :]
        a = face_ref[i : i + 1, :] * el
        local_key = jnp.where(n < el, a + n, -1)
        ghost_key = jnp.where((n >= el) & (n < el + slots), a + n - el, -1)
        cols = slice(i * el, (i + 1) * el)
        onehot[0, :, cols] = (onerow == local_key).astype(F32).astype(BF16)
        onehot[1, :, cols] = (onerow == ghost_key).astype(F32).astype(BF16)
    send_rows = lax.broadcasted_iota(jnp.int32, (el, slots), 0)
    send_hot = jnp.transpose((send_rows == send_ref[...]).astype(F32)).astype(BF16)

    fb = proj_ref.shape[0]
    kf = -(-fb // 16) * 16
    w_pred = jnp.concatenate([weights(-stiff_ref[d], kb) for d in range(3)], axis=0)
    w_vol = jnp.concatenate(
        [weights(jnp.transpose(stiff_ref[d]), kb) for d in range(3)], axis=0
    )
    by_face = [grown(proj_ref[:, i, :], fp) for i in range(nfaces)]
    w_proj = weights(jnp.transpose(jnp.concatenate(by_face, axis=0)), kb)
    by_face = [grown(lift_ref[:, i, :], fp) for i in range(nfaces)]
    w_lift = weights(jnp.concatenate(by_face, axis=0), nfaces * fp)
    w_rot = jnp.concatenate(
        [
            grown(weights(jnp.transpose(rot_ref[h]), kf), fp)
            for h in range(rot_ref.shape[0])
        ],
        axis=0,
    )

    def send(x, data):
        pad = sendbuf.shape[3] - nf * nb
        full = jnp.concatenate([data, jnp.zeros((pad, el), F32)], axis=0)
        hi, lo = split(full)
        nt = (((1,), (1,)), ((), ()))
        out = lax.dot_general(send_hot, hi, nt, preferred_element_type=F32)
        out = out + lax.dot_general(send_hot, lo, nt, preferred_element_type=F32)
        sendbuf[x] = out.reshape(peers, blk, sendbuf.shape[3])
        if x == 0:
            waits = (subs - 1) + jnp.where(slab > 0, subs, 0) + jnp.where(slab < slabs - 1, subs, 0)
            pl.semaphore_wait(barrier, waits)
        each_peer(lambda t, r, there: copy_to(x, t, r, there).start())

    def fields(load):
        return tripled(jnp.concatenate([load(q) for q in range(nf)], axis=1))

    def vol_part(source, p0, width, init):
        acc = list(init)
        for d in range(3):
            for q in range(nf):
                m = source(d, q).reshape(nb // 8, 8, el)
                for k in range(width):
                    acc[k] = acc[k] + m * star[d, q * nf + p0 + k][None]
        return acc

    step_p = 3

    def spread(slot, q0, res, width):
        for k in range(width):
            for d in range(3):
                moved[slot, d * nf + q0 + k] = res[d * nb : (d + 1) * nb, k * el : (k + 1) * el]

    def predict(load, later_out, first_out):
        zero = jnp.zeros((kb - nb, el), F32)
        for q in range(nf):
            x = load(q)
            first_out[q] = jnp.concatenate([x, zero], axis=0)
            if later_out is not None:
                later_out[q] = jnp.concatenate([x, zero], axis=0)
        for q0 in range(0, nf, step_p):
            rhs = tripled(
                jnp.concatenate([first_out[q0 + k] for k in range(step_p)], axis=1)
            )
            spread(0, q0, dot(w_pred, rhs), step_p)

        def order_step(k, carry):
            fact, power = carry
            fact = fact / (k + 2).astype(F32)
            power = power * 2.0
            c2 = (2.0 * power - 1.0) * fact
            now = lax.rem(k, 2)
            nxt = 1 - now
            for p0 in range(0, nf, step_p):
                zeros = [jnp.zeros((nb // 8, 8, el), F32)] * step_p
                acc = vol_part(lambda d, q: moved[now, d * nf + q], p0, step_p, zeros)
                flat = [a.reshape(nb, el) for a in acc]
                for j in range(step_p):
                    first_out[p0 + j, :nb] += fact * flat[j]
                    if later_out is not None:
                        later_out[p0 + j, :nb] += c2 * flat[j]
                rhs = tripled(
                    jnp.concatenate(
                        [jnp.concatenate([a, zero], axis=0) for a in flat], axis=1
                    )
                )
                spread(nxt, p0, dot(w_pred, rhs), step_p)
            return fact, power

        lax.fori_loop(0, ORDER - 1, order_step, (jnp.float32(1.0), jnp.float32(1.0)))

    def gather(load, which):
        lhs = jnp.concatenate(
            [
                jnp.concatenate([load(a, q) for a in range(4)], axis=1)
                for q in range(nf)
            ],
            axis=0,
        )
        hi, lo = split(lhs)
        return dot(hi, onehot[which]) + dot(lo, onehot[which])

    def ghost_fields(x):
        g = ghost[x].reshape(slots, ghost.shape[3])
        g = jnp.concatenate([g, jnp.zeros((el - slots, ghost.shape[3]), F32)], axis=0)
        t = jnp.transpose(g)
        zero = jnp.zeros((kb - nb, el), F32)
        return lambda q: jnp.concatenate([t[q * nb : (q + 1) * nb], zero], axis=0)

    def face_sum(coef, source, i, p):
        acc = jnp.zeros((fp, el), F32)
        for q in range(nf):
            acc = acc + source(i, q) * coef[q, p, i : i + 1, :]
        return acc

    def update(x, source_proj, own_proj, out):
        near = gather(source_proj, 0)
        for i in range(nfaces):
            for p in range(nf):
                solved[i * fp : (i + 1) * fp, p * el : (p + 1) * el] = face_sum(
                    own_ref, own_proj, i, p
                )
        each_peer(lambda t, r, there: arrival(x, t, r, there).wait_recv())
        res = dot(w_proj, fields(ghost_fields(x)))
        near = near + gather(
            lambda a, q: res[a * fp : (a + 1) * fp, q * el : (q + 1) * el], 1
        )
        zero = jnp.zeros((kf - fp, el), F32)
        for i in range(nfaces):
            turn = turn_ref[i : i + 1, :]
            rhs = tripled(
                jnp.concatenate(
                    [
                        jnp.concatenate(
                            [near[q * fp : (q + 1) * fp, i * el : (i + 1) * el], zero], axis=0
                        )
                        for q in range(nf)
                    ],
                    axis=1,
                )
            )
            turned = dot(w_rot, rhs)
            for q in range(nf):
                cols = slice(q * el, (q + 1) * el)
                got = jnp.where(
                    turn == 0,
                    turned[:fp, cols],
                    jnp.where(turn == 1, turned[fp : 2 * fp, cols], turned[2 * fp :, cols]),
                )
                if x == 0:
                    chosen_first[i * nf + q] = got
                else:
                    got = got + jnp.where(is_fine, 0.0, chosen_first[i * nf + q])
                chosen[i * nf + q] = got
            for p in range(nf):
                cols = slice(p * el, (p + 1) * el)
                solved[i * fp : (i + 1) * fp, cols] += face_sum(
                    across_ref, lambda i, q: chosen[i * nf + q], i, p
                )
        lifted = dot(w_lift, tripled(solved[...]))
        for p in range(nf):
            out[p, :nb] = out[p, :nb] - lifted[:, p * el : (p + 1) * el]

    is_fine = cluster_ref[...] == 0

    predict(lambda q: dof_ref[q], second, first)
    send(0, jnp.concatenate([first[q, :nb] for q in range(nf)], axis=0))

    def volume_into(base, out):
        for p0 in range(0, nf, step_p):
            init = [base(p0 + k).reshape(nb // 8, 8, el) for k in range(step_p)]
            acc = vol_part(lambda d, q: moved[0, d * nf + q], p0, step_p, init)
            for k in range(step_p):
                out[p0 + k, :nb] = acc[k].reshape(nb, el)

    rhs = fields(lambda q: first[q])
    spread(0, 0, dot(w_vol, rhs), nf)
    res = dot(w_proj, rhs)
    for i in range(nfaces):
        for q in range(nf):
            r0 = i * fp
            proj[0, i * nf + q] = res[r0 : r0 + fp, q * el : (q + 1) * el]
    volume_into(lambda p: dof_ref[p], stepped)
    pick = lambda s: lambda i, q: proj[s, i * nf + q]
    update(0, pick(0), pick(0), stepped)

    predict(lambda q: stepped[q, :nb], None, state)
    for q in range(nf):
        second[q] = jnp.where(is_fine, state[q], second[q])
    send(1, jnp.concatenate([second[q, :nb] for q in range(nf)], axis=0))

    res = dot(w_proj, fields(lambda q: second[q]))
    for i in range(nfaces):
        for q in range(nf):
            later = res[i * fp : (i + 1) * fp, q * el : (q + 1) * el]
            proj[1, i * nf + q] = later
            proj[2, i * nf + q] = later + jnp.where(is_fine, 0.0, proj[0, i * nf + q])
    for q in range(nf):
        state[q] = second[q] + jnp.where(is_fine, 0.0, first[q])
    spread(0, 0, dot(w_vol, fields(lambda q: state[q])), nf)
    volume_into(lambda p: jnp.where(is_fine, stepped[p, :nb], dof_ref[p]), out_ref)
    update(1, pick(1), pick(2), out_ref)

    for x in range(2):
        each_peer(lambda t, r, there: copy_to(x, t, r, there).wait_send())


def local(
    slabs,
    subs,
    dof_state,
    stiffness,
    face_proj,
    face_lift,
    face_rotate,
    jacobians,
    material,
    inv_jacobian,
    flux_own,
    flux_across,
    cluster,
    neighbour,
    across_face,
    rotation,
    send_list,
):
    nb, nf, el = dof_state.shape
    nfaces, fb, _ = face_proj.shape
    nmat = jacobians.shape[0]
    blk = send_list.shape[0] // (3 * subs)
    fp = -(-fb // 8) * 8
    kb = -(-nb // 16) * 16
    lanes = -(-nf * nb // 128) * 128
    vmem = pl.BlockSpec(memory_space=pltpu.VMEM)
    args = (
        jnp.transpose(dof_state, (1, 0, 2)),
        stiffness,
        jnp.transpose(face_proj, (1, 0, 2)),
        jnp.transpose(face_lift, (2, 0, 1)),
        face_rotate,
        jnp.transpose(jacobians, (2, 3, 1, 0)),
        inv_jacobian,
        jnp.transpose(flux_own, (1, 2, 0, 3)),
        jnp.transpose(flux_across, (1, 2, 0, 3)),
        material.reshape(1, el),
        cluster.reshape(1, el),
        neighbour,
        across_face,
        rotation,
        send_list.reshape(1, send_list.shape[0]),
    )
    out = pl.pallas_call(
        functools.partial(kernel, (nb, nf, el, fp, nfaces, slabs, subs, blk)),
        out_shape=jax.ShapeDtypeStruct((nf, nb, el), F32),
        in_specs=[pl.BlockSpec(memory_space=pltpu.HBM)] * 15,
        out_specs=vmem,
        scratch_shapes=[pltpu.VMEM(x.shape, x.dtype) for x in args]
        + [
            pltpu.VMEM((2, 3 * subs, blk, lanes), F32),
            pltpu.VMEM((2, 3 * subs, blk, lanes), F32),
            pltpu.VMEM((3, nf * nf, 8, el), F32),
            pltpu.VMEM((nf, kb, el), F32),
            pltpu.VMEM((2, 3 * nf, nb, el), F32),
            pltpu.VMEM((3, nfaces * nf, fp, el), F32),
            pltpu.VMEM((nf, kb, el), F32),
            pltpu.VMEM((nf, kb, el), F32),
            pltpu.VMEM((nf, nb, el), F32),
            pltpu.VMEM((nfaces * nf, fp, el), F32),
            pltpu.VMEM((nfaces * nf, fp, el), F32),
            pltpu.VMEM((nfaces * fp, nf * el), F32),
            pltpu.VMEM((2, 4 * el, nfaces * el), BF16),
            pltpu.SemaphoreType.DMA((2, 3 * subs)),
            pltpu.SemaphoreType.DMA((2, 3 * subs)),
            pltpu.SemaphoreType.DMA((len(args),)),
        ],
        compiler_params=pltpu.CompilerParams(
            collective_id=0, has_side_effects=True, vmem_limit_bytes=64 * 2**20
        ),
    )(
        *args,
    )
    return jnp.transpose(out, (1, 0, 2))


def solution(mesh):
    split_all = ("dom", "sub")
    in_specs = (
        P(None, None, split_all),
        P(),
        P(),
        P(),
        P(),
        P(),
        P(split_all),
        P(None, None, split_all),
        P(None, None, None, split_all),
        P(None, None, None, split_all),
        P(split_all),
        P(None, split_all),
        P(None, split_all),
        P(None, split_all),
        P(split_all),
    )
    return jax.shard_map(
        functools.partial(local, mesh.shape["dom"], mesh.shape["sub"]),
        mesh=mesh,
        in_specs=in_specs,
        out_specs=P(None, None, split_all),
        check_vma=False,
    )
```

```python
import functools
import math

import jax
import jax.numpy as jnp
from jax import lax
from jax.experimental import pallas as pl
from jax.experimental.pallas import tpu as pltpu
from jax.sharding import PartitionSpec as P

ORDER = 6
MESH = pl.DeviceIdType.MESH
F32 = jnp.float32
BF16 = jnp.bfloat16


def split(x):
    hi = x.astype(BF16)
    return hi, (x - hi.astype(F32)).astype(BF16)


def tripled(x):
    hi, lo = split(x)
    return jnp.concatenate([hi, lo, hi], axis=0)


def grown(x, rows):
    if x.shape[0] == rows:
        return x
    return jnp.concatenate([x, jnp.zeros((rows - x.shape[0], x.shape[1]), x.dtype)], axis=0)


def weights(x, depth):
    x = grown(x, depth)
    w = jnp.transpose(jnp.concatenate([x, x, x], axis=0))
    hi, lo = split(w)
    lane = lax.broadcasted_iota(jnp.int32, w.shape, 1)
    return jnp.where(lane < 2 * depth, hi.astype(F32), lo.astype(F32)).astype(BF16)


def dot(a, b):
    return jnp.dot(a, b, preferred_element_type=F32)


def kernel(dims, *refs):
    hbm, refs = refs[:15], refs[15:]
    out_ref, held, refs = refs[0], refs[1:16], refs[16:]
    (
        dof_ref,
        stiff_ref,
        proj_ref,
        lift_ref,
        rot_ref,
        table_ref,
        inv_ref,
        own_ref,
        across_ref,
        material_ref,
        cluster_ref,
        neighbour_ref,
        face_ref,
        turn_ref,
        send_ref,
    ) = held
    (
        sendbuf,
        ghost,
        star,
        state,
        moved,
        moved_b,
        proj,
        first,
        second,
        stepped,
        chosen,
        chosen_first,
        solved,
        onehot,
        send_sem,
        recv_sem,
        load_sem,
    ) = refs
    loads = [
        pltpu.make_async_copy(hbm[k], held[k], load_sem.at[k]) for k in range(15)
    ]
    for k in (5, 9, 6, 1, 0, 14, 10, 2, 11, 12, 13, 7, 3, 4, 8):
        loads[k].start()

    def ready(*which):
        for k in which:
            loads[k].wait()

    nb, nf, el, fp, nfaces, slabs, subs, blk = dims
    kb = state.shape[1]
    peers = 3 * subs
    slots = peers * blk
    slab = lax.axis_index("dom")
    sub = lax.axis_index("sub")
    barrier = pltpu.get_barrier_semaphore()

    def each_peer(act):
        for t in (-1, 0, 1):
            for r in range(subs):
                there = slab + t
                valid = (there >= 0) & (there < slabs)
                if t == 0:
                    valid = valid & (sub != r)

                @pl.when(valid)
                def _(t=t, r=r, there=there):
                    act(t, r, there)

    ghost[...] = jnp.zeros(ghost.shape, F32)
    each_peer(
        lambda t, r, there: pl.semaphore_signal(
            barrier, inc=1, device_id=(there, r), device_id_type=MESH
        )
    )

    def copy_to(x, t, r, there):
        slot = (1 - t) * subs + sub
        return pltpu.make_async_remote_copy(
            src_ref=sendbuf.at[x, (t + 1) * subs + r],
            dst_ref=ghost.at[x, slot],
            send_sem=send_sem.at[x, (t + 1) * subs + r],
            recv_sem=recv_sem.at[x, slot],
            device_id=(there, r),
            device_id_type=MESH,
        )

    def arrival(x, t, r, there):
        j = (t + 1) * subs + r
        return pltpu.make_async_remote_copy(
            src_ref=sendbuf.at[x, j],
            dst_ref=ghost.at[x, j],
            send_sem=send_sem.at[x, j],
            recv_sem=recv_sem.at[x, j],
            device_id=(there, r),
            device_id_type=MESH,
        )

    ready(5, 9, 6)
    nmat = table_ref.shape[3]
    rows = lax.broadcasted_iota(jnp.int32, (nmat, el), 0)
    picked = (rows == material_ref[...]).astype(F32).astype(BF16)
    per_elem = []
    for c in range(3):
        hi, lo = split(table_ref[:, :, c, :].reshape(nf * nf, nmat))
        per_elem.append(dot(hi, picked) + dot(lo, picked))
    for d in range(3):
        total = inv_ref[0, d : d + 1, :] * per_elem[0]
        for c in range(1, 3):
            total = total + inv_ref[c, d : d + 1, :] * per_elem[c]
        star[d] = jnp.broadcast_to(total[:, None, :], (nf * nf, 8, el))

    ready(14, 1, 0, 10)
    send_rows = lax.broadcasted_iota(jnp.int32, (el, slots), 0)
    send_hot = jnp.transpose((send_rows == send_ref[...]).astype(F32)).astype(BF16)

    w_pred = jnp.concatenate([weights(-stiff_ref[d], kb) for d in range(3)], axis=0)
    def send(x, data):
        pad = sendbuf.shape[3] - nf * nb
        full = jnp.concatenate([data, jnp.zeros((pad, el), F32)], axis=0)
        hi, lo = split(full)
        nt = (((1,), (1,)), ((), ()))
        out = lax.dot_general(send_hot, hi, nt, preferred_element_type=F32)
        out = out + lax.dot_general(send_hot, lo, nt, preferred_element_type=F32)
        sendbuf[x] = out.reshape(peers, blk, sendbuf.shape[3])
        if x == 0:
            waits = (subs - 1) + jnp.where(slab > 0, subs, 0) + jnp.where(slab < slabs - 1, subs, 0)
            pl.semaphore_wait(barrier, waits)
        each_peer(lambda t, r, there: copy_to(x, t, r, there).start())

    def fields(load):
        return tripled(jnp.concatenate([load(q) for q in range(nf)], axis=1))

    def vol_part(source, p0, width, init):
        acc = list(init)
        for q in range(nf):
            for d in range(3):
                m = source[d * nf + q].reshape(nb // 8, 8, el)
                for k in range(width):
                    acc[k] = acc[k] + m * star[d, q * nf + p0 + k][None]
        return acc

    chunks = [(p0, min(4, nf - p0)) for p0 in range(0, nf, 4)]

    def spread(target, q0, res, width):
        for k in range(width):
            for d in range(3):
                target[d * nf + q0 + k] = res[d * nb : (d + 1) * nb, k * el : (k + 1) * el]

    def predict(load, later_out, first_out):
        zero = jnp.zeros((kb - nb, el), F32)
        for q in range(nf):
            x = grown(load(q), kb)
            first_out[q] = x
            if later_out is not None:
                later_out[q] = x
        for q0, width in chunks:
            rhs = tripled(
                jnp.concatenate([grown(load(q0 + k), kb) for k in range(width)], axis=1)
            )
            spread(moved, q0, dot(w_pred, rhs), width)

        def order_step(k, carry, now, nxt):
            fact, power = carry
            fact = fact / (k + 2).astype(F32)
            power = power * 2.0
            c2 = (2.0 * power - 1.0) * fact
            for p0, width in chunks:
                zeros = [jnp.zeros((nb // 8, 8, el), F32)] * width
                acc = vol_part(now, p0, width, zeros)
                flat = [a.reshape(nb, el) for a in acc]
                for j in range(width):
                    first_out[p0 + j, :nb] += fact * flat[j]
                    if later_out is not None:
                        later_out[p0 + j, :nb] += c2 * flat[j]
                if nxt is not None:
                    rhs = tripled(
                        jnp.concatenate([grown(a, kb) for a in flat], axis=1)
                    )
                    spread(nxt, p0, dot(w_pred, rhs), width)
            return fact, power

        def pair(h, carry):
            carry = order_step(2 * h, carry, moved, moved_b)
            return order_step(2 * h + 1, carry, moved_b, moved)

        steps = ORDER - 1
        carry = (jnp.float32(1.0), jnp.float32(1.0))
        carry = lax.fori_loop(0, steps // 2, pair, carry)
        order_step(jnp.int32(steps - 1), carry, moved, None)

    def gather(load, which):
        lhs = jnp.concatenate(
            [
                jnp.concatenate([load(a, q) for a in range(4)], axis=1)
                for q in range(nf)
            ],
            axis=0,
        )
        hi, lo = split(lhs)
        return dot(hi, onehot[which]) + dot(lo, onehot[which])

    def ghost_fields(x):
        g = ghost[x].reshape(slots, ghost.shape[3])
        g = jnp.concatenate([g, jnp.zeros((el - slots, ghost.shape[3]), F32)], axis=0)
        t = jnp.transpose(g)
        zero = jnp.zeros((kb - nb, el), F32)
        return lambda q: jnp.concatenate([t[q * nb : (q + 1) * nb], zero], axis=0)

    def face_sums(coef, source, i):
        acc = [jnp.zeros((fp, el), F32)] * nf
        for q in range(nf):
            data = source(i, q)
            for p in range(nf):
                acc[p] = acc[p] + data * coef[q, p, i : i + 1, :]
        return acc

    def update(x, source_proj, own_proj, out):
        near = gather(source_proj, 0)
        if x == 0:
            ready(7)
        for i in range(nfaces):
            sums = face_sums(own_ref, own_proj, i)
            for p in range(nf):
                solved[i * fp : (i + 1) * fp, p * el : (p + 1) * el] = sums[p]
        if x == 0:
            ready(8)
        each_peer(lambda t, r, there: arrival(x, t, r, there).wait_recv())
        res = dot(w_proj, fields(ghost_fields(x)))
        near = near + gather(
            lambda a, q: res[a * fp : (a + 1) * fp, q * el : (q + 1) * el], 1
        )
        zero = jnp.zeros((-(-proj_ref.shape[0] // 16) * 16 - fp, el), F32)
        for i in range(nfaces):
            turn = turn_ref[i : i + 1, :]
            rhs = tripled(
                jnp.concatenate(
                    [
                        jnp.concatenate(
                            [near[q * fp : (q + 1) * fp, i * el : (i + 1) * el], zero], axis=0
                        )
                        for q in range(nf)
                    ],
                    axis=1,
                )
            )
            turned = dot(w_rot, rhs)
            for q in range(nf):
                cols = slice(q * el, (q + 1) * el)
                got = jnp.where(
                    turn == 0,
                    turned[:fp, cols],
                    jnp.where(turn == 1, turned[fp : 2 * fp, cols], turned[2 * fp :, cols]),
                )
                if x == 0:
                    chosen_first[i * nf + q] = got
                else:
                    got = got + jnp.where(is_fine, 0.0, chosen_first[i * nf + q])
                chosen[i * nf + q] = got
            sums = face_sums(across_ref, lambda i, q: chosen[i * nf + q], i)
            for p in range(nf):
                solved[i * fp : (i + 1) * fp, p * el : (p + 1) * el] += sums[p]
        lifted = dot(w_lift, tripled(solved[...]))
        for p in range(nf):
            out[p, :nb] = out[p, :nb] - lifted[:, p * el : (p + 1) * el]

    is_fine = cluster_ref[...] == 0

    predict(lambda q: dof_ref[q], second, first)
    send(0, jnp.concatenate([first[q, :nb] for q in range(nf)], axis=0))

    ready(2, 11, 12, 13, 3, 4)
    onerow = lax.broadcasted_iota(jnp.int32, (4 * el, el), 0)
    for i in range(nfaces):
        n = neighbour_ref[i : i + 1, :]
        a = face_ref[i : i + 1, :] * el
        local_key = jnp.where(n < el, a + n, -1)
        ghost_key = jnp.where((n >= el) & (n < el + slots), a + n - el, -1)
        cols = slice(i * el, (i + 1) * el)
        onehot[0, :, cols] = (onerow == local_key).astype(F32).astype(BF16)
        onehot[1, :, cols] = (onerow == ghost_key).astype(F32).astype(BF16)
    fb = proj_ref.shape[0]
    kf = -(-fb // 16) * 16
    w_vol = jnp.concatenate(
        [weights(jnp.transpose(stiff_ref[d]), kb) for d in range(3)], axis=0
    )
    by_face = [grown(proj_ref[:, i, :], fp) for i in range(nfaces)]
    w_proj = weights(jnp.transpose(jnp.concatenate(by_face, axis=0)), kb)
    by_face = [grown(lift_ref[:, i, :], fp) for i in range(nfaces)]
    w_lift = weights(jnp.concatenate(by_face, axis=0), nfaces * fp)
    w_rot = jnp.concatenate(
        [
            grown(weights(jnp.transpose(rot_ref[h]), kf), fp)
            for h in range(rot_ref.shape[0])
        ],
        axis=0,
    )

    def volume_into(base, out):
        for p0, width in chunks:
            init = [base(p0 + k).reshape(nb // 8, 8, el) for k in range(width)]
            acc = vol_part(moved, p0, width, init)
            for k in range(width):
                out[p0 + k, :nb] = acc[k].reshape(nb, el)

    rhs = fields(lambda q: first[q])
    spread(moved, 0, dot(w_vol, rhs), nf)
    res = dot(w_proj, rhs)
    for i in range(nfaces):
        for q in range(nf):
            r0 = i * fp
            proj[0, i * nf + q] = res[r0 : r0 + fp, q * el : (q + 1) * el]
    volume_into(lambda p: dof_ref[p], stepped)
    pick = lambda s: lambda i, q: proj[s, i * nf + q]
    update(0, pick(0), pick(0), stepped)

    predict(lambda q: stepped[q, :nb], None, state)
    for q in range(nf):
        second[q] = jnp.where(is_fine, state[q], second[q])
    send(1, jnp.concatenate([second[q, :nb] for q in range(nf)], axis=0))

    res = dot(w_proj, fields(lambda q: second[q]))
    for i in range(nfaces):
        for q in range(nf):
            later = res[i * fp : (i + 1) * fp, q * el : (q + 1) * el]
            proj[1, i * nf + q] = later
            proj[2, i * nf + q] = later + jnp.where(is_fine, 0.0, proj[0, i * nf + q])
    for q in range(nf):
        state[q] = second[q] + jnp.where(is_fine, 0.0, first[q])
    spread(moved, 0, dot(w_vol, fields(lambda q: state[q])), nf)
    volume_into(lambda p: jnp.where(is_fine, stepped[p, :nb], dof_ref[p]), out_ref)
    update(1, pick(1), pick(2), out_ref)

    for x in range(2):
        each_peer(lambda t, r, there: copy_to(x, t, r, there).wait_send())


def local(
    slabs,
    subs,
    dof_state,
    stiffness,
    face_proj,
    face_lift,
    face_rotate,
    jacobians,
    material,
    inv_jacobian,
    flux_own,
    flux_across,
    cluster,
    neighbour,
    across_face,
    rotation,
    send_list,
):
    nb, nf, el = dof_state.shape
    nfaces, fb, _ = face_proj.shape
    nmat = jacobians.shape[0]
    blk = send_list.shape[0] // (3 * subs)
    fp = -(-fb // 8) * 8
    kb = -(-nb // 16) * 16
    lanes = -(-nf * nb // 128) * 128
    vmem = pl.BlockSpec(memory_space=pltpu.VMEM)
    args = (
        jnp.transpose(dof_state, (1, 0, 2)),
        stiffness,
        jnp.transpose(face_proj, (1, 0, 2)),
        jnp.transpose(face_lift, (2, 0, 1)),
        face_rotate,
        jnp.transpose(jacobians, (2, 3, 1, 0)),
        inv_jacobian,
        jnp.transpose(flux_own, (1, 2, 0, 3)),
        jnp.transpose(flux_across, (1, 2, 0, 3)),
        material.reshape(1, el),
        cluster.reshape(1, el),
        neighbour,
        across_face,
        rotation,
        send_list.reshape(1, send_list.shape[0]),
    )
    out = pl.pallas_call(
        functools.partial(kernel, (nb, nf, el, fp, nfaces, slabs, subs, blk)),
        out_shape=pltpu.VMEM((nf, nb, el), F32),
        in_specs=[pl.BlockSpec(memory_space=pltpu.HBM)] * 15,
        out_specs=vmem,
        scratch_shapes=[pltpu.VMEM(x.shape, x.dtype) for x in args]
        + [
            pltpu.VMEM((2, 3 * subs, blk, lanes), F32),
            pltpu.VMEM((2, 3 * subs, blk, lanes), F32),
            pltpu.VMEM((3, nf * nf, 8, el), F32),
            pltpu.VMEM((nf, kb, el), F32),
            pltpu.VMEM((3 * nf, nb, el), F32),
            pltpu.VMEM((3 * nf, nb, el), F32),
            pltpu.VMEM((3, nfaces * nf, fp, el), F32),
            pltpu.VMEM((nf, kb, el), F32),
            pltpu.VMEM((nf, kb, el), F32),
            pltpu.VMEM((nf, nb, el), F32),
            pltpu.VMEM((nfaces * nf, fp, el), F32),
            pltpu.VMEM((nfaces * nf, fp, el), F32),
            pltpu.VMEM((nfaces * fp, nf * el), F32),
            pltpu.VMEM((2, 4 * el, nfaces * el), BF16),
            pltpu.SemaphoreType.DMA((2, 3 * subs)),
            pltpu.SemaphoreType.DMA((2, 3 * subs)),
            pltpu.SemaphoreType.DMA((len(args),)),
        ],
        compiler_params=pltpu.CompilerParams(
            collective_id=0, has_side_effects=True, vmem_limit_bytes=48 * 2**20
        ),
    )(
        *[pltpu.with_memory_space_constraint(x, pltpu.HBM) for x in args],
    )
    return jnp.transpose(out, (1, 0, 2))


def solution(mesh):
    split_all = ("dom", "sub")
    in_specs = (
        P(None, None, split_all),
        P(),
        P(),
        P(),
        P(),
        P(),
        P(split_all),
        P(None, None, split_all),
        P(None, None, None, split_all),
        P(None, None, None, split_all),
        P(split_all),
        P(None, split_all),
        P(None, split_all),
        P(None, split_all),
        P(split_all),
    )
    return jax.shard_map(
        functools.partial(local, mesh.shape["dom"], mesh.shape["sub"]),
        mesh=mesh,
        in_specs=in_specs,
        out_specs=P(None, None, split_all),
        check_vma=False,
    )
```

```python
import functools
import math

import jax
import jax.numpy as jnp
from jax import lax
from jax.experimental import pallas as pl
from jax.experimental.pallas import tpu as pltpu
from jax.sharding import PartitionSpec as P

ORDER = 6
MESH = pl.DeviceIdType.MESH
F32 = jnp.float32
BF16 = jnp.bfloat16


def split(x):
    hi = x.astype(BF16)
    return hi, (x - hi.astype(F32)).astype(BF16)


def tripled(x):
    hi, lo = split(x)
    return jnp.concatenate([hi, lo, hi], axis=0)


def grown(x, rows):
    if x.shape[0] == rows:
        return x
    return jnp.concatenate([x, jnp.zeros((rows - x.shape[0], x.shape[1]), x.dtype)], axis=0)


def weights(x, depth):
    x = grown(x, depth)
    w = jnp.transpose(jnp.concatenate([x, x, x], axis=0))
    hi, lo = split(w)
    lane = lax.broadcasted_iota(jnp.int32, w.shape, 1)
    return jnp.where(lane < 2 * depth, hi.astype(F32), lo.astype(F32)).astype(BF16)


def dot(a, b):
    return jnp.dot(a, b, preferred_element_type=F32)


def kernel(dims, *refs):
    hbm, refs = refs[:15], refs[15:]
    out_ref, held, refs = refs[0], refs[1:16], refs[16:]
    (
        dof_ref,
        stiff_ref,
        proj_ref,
        lift_ref,
        rot_ref,
        table_ref,
        inv_ref,
        own_ref,
        across_ref,
        material_ref,
        cluster_ref,
        neighbour_ref,
        face_ref,
        turn_ref,
        send_ref,
    ) = held
    (
        sendbuf,
        ghost,
        star,
        state,
        moved,
        moved_b,
        proj,
        first,
        second,
        stepped,
        chosen,
        chosen_first,
        solved,
        onehot,
        ghost_hot,
        send_sem,
        recv_sem,
        load_sem,
    ) = refs
    loads = [
        pltpu.make_async_copy(hbm[k], held[k], load_sem.at[k]) for k in range(15)
    ]
    for k in (5, 9, 6, 1, 0, 14, 10, 2, 11, 12, 13, 7, 3, 4, 8):
        loads[k].start()

    def ready(*which):
        for k in which:
            loads[k].wait()

    nb, nf, el, fp, nfaces, slabs, subs, blk = dims
    kb = state.shape[1]
    peers = 3 * subs
    slots = peers * blk
    slab = lax.axis_index("dom")
    sub = lax.axis_index("sub")
    barrier = pltpu.get_barrier_semaphore()

    def each_peer(act):
        for t in (-1, 0, 1):
            for r in range(subs):
                there = slab + t
                valid = (there >= 0) & (there < slabs)
                if t == 0:
                    valid = valid & (sub != r)

                @pl.when(valid)
                def _(t=t, r=r, there=there):
                    act(t, r, there)

    ghost[...] = jnp.zeros(ghost.shape, F32)
    each_peer(
        lambda t, r, there: pl.semaphore_signal(
            barrier, inc=1, device_id=(there, r), device_id_type=MESH
        )
    )

    def copy_to(x, t, r, there):
        slot = (1 - t) * subs + sub
        return pltpu.make_async_remote_copy(
            src_ref=sendbuf.at[x, (t + 1) * subs + r],
            dst_ref=ghost.at[x, slot],
            send_sem=send_sem.at[x, (t + 1) * subs + r],
            recv_sem=recv_sem.at[x, slot],
            device_id=(there, r),
            device_id_type=MESH,
        )

    def arrival(x, t, r, there):
        j = (t + 1) * subs + r
        return pltpu.make_async_remote_copy(
            src_ref=sendbuf.at[x, j],
            dst_ref=ghost.at[x, j],
            send_sem=send_sem.at[x, j],
            recv_sem=recv_sem.at[x, j],
            device_id=(there, r),
            device_id_type=MESH,
        )

    ready(5, 9, 6)
    nmat = table_ref.shape[3]
    rows = lax.broadcasted_iota(jnp.int32, (nmat, el), 0)
    picked = (rows == material_ref[...]).astype(F32).astype(BF16)
    per_elem = []
    for c in range(3):
        hi, lo = split(table_ref[:, :, c, :].reshape(nf * nf, nmat))
        per_elem.append(dot(hi, picked) + dot(lo, picked))
    for d in range(3):
        total = inv_ref[0, d : d + 1, :] * per_elem[0]
        for c in range(1, 3):
            total = total + inv_ref[c, d : d + 1, :] * per_elem[c]
        star[d] = jnp.broadcast_to(total[:, None, :], (nf * nf, 8, el))

    ready(14, 1, 0, 10)
    send_rows = lax.broadcasted_iota(jnp.int32, (el, slots), 0)
    send_hot = jnp.transpose((send_rows == send_ref[...]).astype(F32)).astype(BF16)

    w_pred = jnp.concatenate([weights(-stiff_ref[d], kb) for d in range(3)], axis=0)
    def send(x, data):
        pad = sendbuf.shape[3] - nf * nb
        full = jnp.concatenate([data, jnp.zeros((pad, el), F32)], axis=0)
        hi, lo = split(full)
        nt = (((1,), (1,)), ((), ()))
        out = lax.dot_general(send_hot, hi, nt, preferred_element_type=F32)
        out = out + lax.dot_general(send_hot, lo, nt, preferred_element_type=F32)
        sendbuf[x] = out.reshape(peers, blk, sendbuf.shape[3])
        if x == 0:
            waits = (subs - 1) + jnp.where(slab > 0, subs, 0) + jnp.where(slab < slabs - 1, subs, 0)
            pl.semaphore_wait(barrier, waits)
        each_peer(lambda t, r, there: copy_to(x, t, r, there).start())

    def fields(load):
        return tripled(jnp.concatenate([load(q) for q in range(nf)], axis=1))

    def vol_part(source, p0, width, init):
        acc = list(init)
        for q in range(nf):
            for d in range(3):
                m = source[d * nf + q].reshape(nb // 8, 8, el)
                for k in range(width):
                    acc[k] = acc[k] + m * star[d, q * nf + p0 + k][None]
        return acc

    chunks = [(p0, min(4, nf - p0)) for p0 in range(0, nf, 4)]

    def spread(target, q0, res, width):
        for k in range(width):
            for d in range(3):
                target[d * nf + q0 + k] = res[d * nb : (d + 1) * nb, k * el : (k + 1) * el]

    def predict(load, later_out, first_out):
        zero = jnp.zeros((kb - nb, el), F32)
        for q in range(nf):
            x = grown(load(q), kb)
            first_out[q] = x
            if later_out is not None:
                later_out[q] = x
        for q0, width in chunks:
            rhs = tripled(
                jnp.concatenate([grown(load(q0 + k), kb) for k in range(width)], axis=1)
            )
            spread(moved, q0, dot(w_pred, rhs), width)

        def order_step(k, carry, now, nxt):
            fact, power = carry
            fact = fact / (k + 2).astype(F32)
            power = power * 2.0
            c2 = (2.0 * power - 1.0) * fact
            for p0, width in chunks:
                zeros = [jnp.zeros((nb // 8, 8, el), F32)] * width
                acc = vol_part(now, p0, width, zeros)
                flat = [a.reshape(nb, el) for a in acc]
                for j in range(width):
                    first_out[p0 + j, :nb] += fact * flat[j]
                    if later_out is not None:
                        later_out[p0 + j, :nb] += c2 * flat[j]
                if nxt is not None:
                    rhs = tripled(
                        jnp.concatenate([grown(a, kb) for a in flat], axis=1)
                    )
                    spread(nxt, p0, dot(w_pred, rhs), width)
            return fact, power

        def pair(h, carry):
            carry = order_step(2 * h, carry, moved, moved_b)
            return order_step(2 * h + 1, carry, moved_b, moved)

        steps = ORDER - 1
        carry = (jnp.float32(1.0), jnp.float32(1.0))
        carry = lax.fori_loop(0, steps // 2, pair, carry)
        order_step(jnp.int32(steps - 1), carry, moved, None)

    def gather(load, hot):
        lhs = jnp.concatenate(
            [
                jnp.concatenate([load(a, q) for a in range(hot.shape[0] // el)], axis=1)
                for q in range(nf)
            ],
            axis=0,
        )
        rows = -(-nf * fp // 16) * 16
        hi, lo = split(grown(lhs, rows))
        both = dot(jnp.concatenate([hi, lo], axis=0), hot[...])
        return both[: nf * fp] + both[rows : rows + nf * fp]

    def ghost_fields(x):
        g = ghost[x].reshape(slots, ghost.shape[3])
        g = jnp.concatenate([grown(g, el)], axis=0)
        t = jnp.transpose(g)
        zero = jnp.zeros((kb - nb, el), F32)
        return lambda q: jnp.concatenate([t[q * nb : (q + 1) * nb], zero], axis=0)

    def face_sums(coef, source, i):
        acc = [jnp.zeros((fp, el), F32)] * nf
        for q in range(nf):
            data = source(i, q)
            for p in range(nf):
                acc[p] = acc[p] + data * coef[q, p, i : i + 1, :]
        return acc

    def update(x, source_proj, own_proj, out):
        near = gather(source_proj, onehot)
        if x == 0:
            ready(7)
        for i in range(nfaces):
            sums = face_sums(own_ref, own_proj, i)
            for p in range(nf):
                solved[i * fp : (i + 1) * fp, p * el : (p + 1) * el] = sums[p]
        if x == 0:
            ready(8)
        def turn_by(parts, turn):
            rhs = tripled(jnp.concatenate([grown(part, kf) for part in parts], axis=1))
            turned = dot(w_rot, rhs)
            result = []
            for q in range(nf):
                cols = slice(q * el, (q + 1) * el)
                last = jnp.where(turn == 1, turned[fp : 2 * fp, cols], turned[2 * fp :, cols])
                result.append(jnp.where(turn == 0, turned[:fp, cols], last))
            return result

        for i in range(nfaces):
            cols = slice(i * el, (i + 1) * el)
            parts = [near[q * fp : (q + 1) * fp, cols] for q in range(nf)]
            for q, got in enumerate(turn_by(parts, turn_ref[i : i + 1, :])):
                if x == 1:
                    got = got + jnp.where(is_fine, 0.0, chosen_first[i * nf + q])
                chosen[i * nf + q] = got
        each_peer(lambda t, r, there: arrival(x, t, r, there).wait_recv())
        res = dot(w_proj, fields(ghost_fields(x)))
        parts = []
        for q in range(nf):
            part = res[:fp, q * el : (q + 1) * el]
            for a in range(1, nfaces):
                other = res[a * fp : (a + 1) * fp, q * el : (q + 1) * el]
                part = jnp.where(slot_face == a, other, part)
            parts.append(part)
        turned = turn_by(parts, slot_turn)
        came = gather(lambda a, q: turned[q], ghost_hot)
        for i in range(nfaces):
            for q in range(nf):
                got = chosen[i * nf + q]
                got = got + came[q * fp : (q + 1) * fp, i * el : (i + 1) * el]
                chosen[i * nf + q] = got
                if x == 0:
                    chosen_first[i * nf + q] = got
            sums = face_sums(across_ref, lambda i, q: chosen[i * nf + q], i)
            for p in range(nf):
                solved[i * fp : (i + 1) * fp, p * el : (p + 1) * el] += sums[p]
        lifted = dot(w_lift, jnp.concatenate(split(solved[...]), axis=0))
        lifted = lifted[:nb] + lifted[nb:]
        for p in range(nf):
            out[p, :nb] = out[p, :nb] - lifted[:, p * el : (p + 1) * el]

    is_fine = cluster_ref[...] == 0

    predict(lambda q: dof_ref[q], second, first)
    send(0, jnp.concatenate([first[q, :nb] for q in range(nf)], axis=0))

    ready(2, 11, 12, 13, 3, 4)
    ghost_row = lax.broadcasted_iota(jnp.int32, ghost_hot.shape[:1] + (el,), 0)
    onerow = lax.broadcasted_iota(jnp.int32, (4 * el, el), 0)
    for i in range(nfaces):
        n = neighbour_ref[i : i + 1, :]
        a = face_ref[i : i + 1, :] * el
        local_key = jnp.where(n < el, a + n, -1)
        ghost_key = jnp.where((n >= el) & (n < el + slots), n - el, -1)
        cols = slice(i * el, (i + 1) * el)
        onehot[:, cols] = (onerow == local_key).astype(F32).astype(BF16)
        ghost_hot[:, cols] = (ghost_row == ghost_key).astype(F32).astype(BF16)
    fb = proj_ref.shape[0]
    kf = -(-fb // 16) * 16
    keys = jnp.concatenate(
        [
            jnp.concatenate([ref[i : i + 1, :] for i in range(nfaces)], axis=1)
            for ref in (face_ref, turn_ref)
        ],
        axis=0,
    )
    slot_keys = lax.dot_general(
        grown(keys.astype(F32), 16).astype(BF16),
        ghost_hot[...],
        (((1,), (1,)), ((), ())),
        preferred_element_type=F32,
    )
    slot_face, slot_turn = slot_keys[0:1], slot_keys[1:2]

    w_vol = jnp.concatenate(
        [weights(jnp.transpose(stiff_ref[d]), kb) for d in range(3)], axis=0
    )
    by_face = [grown(proj_ref[:, i, :], fp) for i in range(nfaces)]
    w_proj = weights(jnp.transpose(jnp.concatenate(by_face, axis=0)), kb)
    by_face = [grown(lift_ref[:, i, :], fp) for i in range(nfaces)]
    lift = jnp.concatenate(by_face, axis=0)
    hi, lo = split(jnp.transpose(jnp.concatenate([lift, lift], axis=0)))
    lane = lax.broadcasted_iota(jnp.int32, lo.shape, 1)
    lo = jnp.where(lane < nfaces * fp, lo.astype(F32), 0.0)
    w_lift = jnp.concatenate([hi.astype(F32), lo], axis=0).astype(BF16)
    w_rot = jnp.concatenate(
        [
            grown(weights(jnp.transpose(rot_ref[h]), kf), fp)
            for h in range(rot_ref.shape[0])
        ],
        axis=0,
    )

    def volume_into(base, out):
        for p0, width in chunks:
            init = [base(p0 + k).reshape(nb // 8, 8, el) for k in range(width)]
            acc = vol_part(moved, p0, width, init)
            for k in range(width):
                out[p0 + k, :nb] = acc[k].reshape(nb, el)

    rhs = fields(lambda q: first[q])
    spread(moved, 0, dot(w_vol, rhs), nf)
    res = dot(w_proj, rhs)
    for i in range(nfaces):
        for q in range(nf):
            r0 = i * fp
            proj[0, i * nf + q] = res[r0 : r0 + fp, q * el : (q + 1) * el]
    volume_into(lambda p: dof_ref[p], stepped)
    pick = lambda s: lambda i, q: proj[s, i * nf + q]
    update(0, pick(0), pick(0), stepped)

    predict(lambda q: stepped[q, :nb], None, state)
    for q in range(nf):
        second[q] = jnp.where(is_fine, state[q], second[q])
    send(1, jnp.concatenate([second[q, :nb] for q in range(nf)], axis=0))

    res = dot(w_proj, fields(lambda q: second[q]))
    for i in range(nfaces):
        for q in range(nf):
            later = res[i * fp : (i + 1) * fp, q * el : (q + 1) * el]
            proj[1, i * nf + q] = later
            proj[2, i * nf + q] = later + jnp.where(is_fine, 0.0, proj[0, i * nf + q])
    for q in range(nf):
        state[q] = second[q] + jnp.where(is_fine, 0.0, first[q])
    spread(moved, 0, dot(w_vol, fields(lambda q: state[q])), nf)
    volume_into(lambda p: jnp.where(is_fine, stepped[p, :nb], dof_ref[p]), out_ref)
    update(1, pick(1), pick(2), out_ref)

    for x in range(2):
        each_peer(lambda t, r, there: copy_to(x, t, r, there).wait_send())


def local(
    slabs,
    subs,
    dof_state,
    stiffness,
    face_proj,
    face_lift,
    face_rotate,
    jacobians,
    material,
    inv_jacobian,
    flux_own,
    flux_across,
    cluster,
    neighbour,
    across_face,
    rotation,
    send_list,
):
    nb, nf, el = dof_state.shape
    nfaces, fb, _ = face_proj.shape
    nmat = jacobians.shape[0]
    blk = send_list.shape[0] // (3 * subs)
    fp = -(-fb // 8) * 8
    kb = -(-nb // 16) * 16
    lanes = -(-nf * nb // 128) * 128
    vmem = pl.BlockSpec(memory_space=pltpu.VMEM)
    args = (
        jnp.transpose(dof_state, (1, 0, 2)),
        stiffness,
        jnp.transpose(face_proj, (1, 0, 2)),
        jnp.transpose(face_lift, (2, 0, 1)),
        face_rotate,
        jnp.transpose(jacobians, (2, 3, 1, 0)),
        inv_jacobian,
        jnp.transpose(flux_own, (1, 2, 0, 3)),
        jnp.transpose(flux_across, (1, 2, 0, 3)),
        material.reshape(1, el),
        cluster.reshape(1, el),
        neighbour,
        across_face,
        rotation,
        send_list.reshape(1, send_list.shape[0]),
    )
    out = pl.pallas_call(
        functools.partial(kernel, (nb, nf, el, fp, nfaces, slabs, subs, blk)),
        out_shape=pltpu.VMEM((nf, nb, el), F32),
        in_specs=[pl.BlockSpec(memory_space=pltpu.HBM)] * 15,
        out_specs=vmem,
        scratch_shapes=[pltpu.VMEM(x.shape, x.dtype) for x in args]
        + [
            pltpu.VMEM((2, 3 * subs, blk, lanes), F32),
            pltpu.VMEM((2, 3 * subs, blk, lanes), F32),
            pltpu.VMEM((3, nf * nf, 8, el), F32),
            pltpu.VMEM((nf, kb, el), F32),
            pltpu.VMEM((3 * nf, nb, el), F32),
            pltpu.VMEM((3 * nf, nb, el), F32),
            pltpu.VMEM((3, nfaces * nf, fp, el), F32),
            pltpu.VMEM((nf, kb, el), F32),
            pltpu.VMEM((nf, kb, el), F32),
            pltpu.VMEM((nf, nb, el), F32),
            pltpu.VMEM((nfaces * nf, fp, el), F32),
            pltpu.VMEM((nfaces * nf, fp, el), F32),
            pltpu.VMEM((nfaces * fp, nf * el), F32),
            pltpu.VMEM((4 * el, nfaces * el), BF16),
            pltpu.VMEM((el, nfaces * el), BF16),
            pltpu.SemaphoreType.DMA((2, 3 * subs)),
            pltpu.SemaphoreType.DMA((2, 3 * subs)),
            pltpu.SemaphoreType.DMA((len(args),)),
        ],
        compiler_params=pltpu.CompilerParams(
            collective_id=0, has_side_effects=True, vmem_limit_bytes=48 * 2**20
        ),
    )(
        *[pltpu.with_memory_space_constraint(x, pltpu.HBM) for x in args],
    )
    return jnp.transpose(out, (1, 0, 2))


def solution(mesh):
    split_all = ("dom", "sub")
    in_specs = (
        P(None, None, split_all),
        P(),
        P(),
        P(),
        P(),
        P(),
        P(split_all),
        P(None, None, split_all),
        P(None, None, None, split_all),
        P(None, None, None, split_all),
        P(split_all),
        P(None, split_all),
        P(None, split_all),
        P(None, split_all),
        P(split_all),
    )
    return jax.shard_map(
        functools.partial(local, mesh.shape["dom"], mesh.shape["sub"]),
        mesh=mesh,
        in_specs=in_specs,
        out_specs=P(None, None, split_all),
        check_vma=False,
    )
```
